32 devices in a mesh: grp: 2 (over x), tm: 16 (over z, y, core).
Axes of the slice: x: 2, y: 2, z: 4, core: 2. Of those that a mesh axis runs over, the one named last changes fastest.
Arguments:
- launch: float32 [2, 32, 16384], P(None, None, ('grp', 'tm')), parts along dimension 2, may hold values from -6 to 6
- target: float32 [2, 32, 16384], P(None, None, ('grp', 'tm')), parts along dimension 2, may hold values from -4 to 4
- taps: float32 [2, 32, 32, 64], replicated, may hold values from -0.09375 to 0.09375
- coupling: float32 [32, 32], replicated, may hold values from 0.004 to 0.03
- delay: float32 [32], replicated, may hold values from -48 to 48
- curv: float32 [32], replicated, may hold values from -300 to 300
Outputs:
- misfit: float32 [2, 32, 16384], P(None, None, ('grp', 'tm')), parts along dimension 2
- launch_grad: float32 [2, 32, 16384], P(None, None, ('grp', 'tm')), parts along dimension 2
- tap_grad: float32 [4, 32, 32, 64], P('grp'), parts along dimension 0
The draws below stay inside these ranges and needn't reach their ends.
There are 2 independent parts, one for each index of `grp`. The reference program is written for one: setup_inputs(seed, part) draws one part's arguments, and reference() takes and returns one part's arrays. A program takes and returns all parts, laid end to end along the dimension named above; an argument that names none is the same for every part. Nothing has to cross between parts.
All inputs are finite; a program needn't handle non-finite values.
Results may differ from the reference program's by a relative error of at most 0.00028.
Values sent between devices are 32-bit elements; how exact they have to be, the bound alone decides.
A program may use at most 128 MiB of HBM per device.

```python
import math
import jax
import jax.numpy as jnp
from jax import lax

M = 32
TAPS = 64
WIN = 8192
NT = 8192


def steps_of(rng, shape, cuts, least, largest):
    loudness, own = 1.0, jax.random.fold_in(rng, 6)
    for position, parts in cuts:
        steps = jnp.exp(jax.random.uniform(jax.random.fold_in(own, position), (parts,), jnp.float32, least / len(cuts), largest / len(cuts)))
        loudness = loudness * jnp.repeat(steps, shape[position] // parts).reshape([-1 if axis == position else 1 for axis in range(len(shape))])
    return loudness


def scatter_about(rng, extent, scale, limit, shards=(), kind=jnp.bfloat16):
    array = jax.random.normal(rng, extent, jnp.float32) * scale
    if len(shards) > 0:
        array = steps_of(rng, extent, shards, -0.22, 0.18) * array
    return jnp.clip(array, min=-limit, max=limit).astype(kind)


def setup_inputs(seed: int = 0, part: int = 0) -> dict:
    seeds = jax.random.split(jax.random.key(seed), 7)
    part_keys = jax.random.split(jax.random.fold_in(seeds[6], part), 7)
    launch = scatter_about(part_keys[0], (2, M, NT), 1.0, 6.0, ((2, 16),), jnp.float32)
    target = scatter_about(part_keys[1], (2, M, NT), 0.5, 4.0, ((2, 16),), jnp.float32)
    taps = scatter_about(seeds[2], (2, M, M, TAPS), (2 * M * TAPS) ** -0.5, 0.09375, (), jnp.float32)
    coupling = jnp.clip(jax.random.uniform(seeds[3], (M, M), jnp.float32, 0.004, 0.03), 0.004, 0.03)
    delay = jnp.clip(jax.random.uniform(seeds[4], (M,), jnp.float32, -48.0, 48.0), -48.0, 48.0)
    curv = jnp.clip(jax.random.uniform(seeds[5], (M,), jnp.float32, -300.0, 300.0), -300.0, 300.0)
    return {"launch": launch, "target": target, "taps": taps, "coupling": coupling, "delay": delay, "curv": curv}


def disperse(field, delay, curv, sign):
    wave = field[0] + 1j * field[1]
    spec = jnp.fft.fft(wave, axis=-1)
    index = jnp.arange(NT)
    centred = jnp.where(index < NT // 2, index, index - NT).astype(field.dtype) / NT
    phase = 2.0 * math.pi * (delay[:, None] * centred[None, :] + curv[:, None] * centred[None, :] * centred[None, :])
    spec = spec * (jnp.cos(phase) + sign * 1j * jnp.sin(phase))
    wave = jnp.fft.ifft(spec, axis=-1)
    return jnp.stack([jnp.real(wave), jnp.imag(wave)]).astype(field.dtype)

def nonlinear(field, coupling):
    power = field[0] * field[0] + field[1] * field[1]
    angle = jnp.dot(coupling, power, precision=lax.Precision.HIGHEST)
    cosine = jnp.cos(angle)
    sine = jnp.sin(angle)
    return jnp.stack([field[0] * cosine - field[1] * sine, field[0] * sine + field[1] * cosine])

def kernel_of(taps):
    upper = jnp.concatenate([taps[0], -taps[1]], axis=1)
    lower = jnp.concatenate([taps[1], taps[0]], axis=1)
    return jnp.concatenate([upper, lower], axis=0)

def filtered(field, taps):
    count = NT // WIN
    blocks = field.reshape(2 * M, count, WIN).transpose(1, 0, 2)
    out = lax.conv_general_dilated(blocks, kernel_of(taps), (1,), [(TAPS - 1, 0)], dimension_numbers=('NCH', 'OIH', 'NCH'), precision=lax.Precision.HIGHEST)
    return out.transpose(1, 0, 2).reshape(2, M, NT)

def reference(launch, target, taps, coupling, delay, curv):

    def forward(start, coeffs):
        moved = disperse(start, delay, curv, 1.0)
        return filtered(nonlinear(moved, coupling), coeffs)
    output, pullback = jax.vjp(forward, launch, taps)
    misfit = output - target
    launch_grad, coeff_grad = pullback(misfit)
    return (misfit, launch_grad, coeff_grad / math.sqrt(NT))
```

```python
import functools
import math

import jax
import jax.numpy as jnp
import ml_dtypes
import numpy as np
from jax import lax
from jax.experimental import pallas as pl
from jax.experimental.pallas import tpu as pltpu
from jax.sharding import PartitionSpec as P


WIN = 8192


def passed_along(block, axis, distance):
    devices = range(lax.axis_size(axis))
    route = [(i - distance, i) for i in devices if i - distance in devices]
    return lax.ppermute(block, axis, route)


def tables(rows, cols, modulus):
    left = jnp.arange(rows, dtype=jnp.int32)[:, None]
    right = jnp.arange(cols, dtype=jnp.int32)[None, :]
    angle = (left * right % modulus).astype(jnp.float32) * (2.0 * math.pi / modulus)
    return (jnp.cos(angle), jnp.sin(angle))


def first_tables(mine, parts, block, total):
    length = parts * block
    index = jnp.arange(length, dtype=jnp.int32)
    outer = index // block
    inner = index % block
    sample = outer[:, None] * length + mine * block + inner[:, None]
    angle = (outer[None, :] * sample % total).astype(jnp.float32) * (2.0 * math.pi / total)
    same = (inner[:, None] == inner[None, :]).astype(jnp.float32)
    return (jnp.cos(angle) * same, jnp.sin(angle) * same)


def rotate(real_part, imag_part, cosine, sine, sign):
    return (
        real_part * cosine - sign * imag_part * sine,
        imag_part * cosine + sign * real_part * sine,
    )


def along_time(field, cosine, sine, sign, form):
    high = lax.Precision.HIGHEST
    cos_real = jnp.einsum(form, field[0], cosine, precision=high)
    cos_imag = jnp.einsum(form, field[1], cosine, precision=high)
    sin_real = jnp.einsum(form, field[0], sine, precision=high)
    sin_imag = jnp.einsum(form, field[1], sine, precision=high)
    return jnp.stack([cos_real - sign * sin_imag, cos_imag + sign * sin_real])


def apply_phase(field, freq, total, delay, curv, sign):
    centred = jnp.where(freq < total // 2, freq, freq - total).astype(jnp.float32) / total
    phase = (
        2.0
        * math.pi
        * (delay[:, None] * centred[None, :] + curv[:, None] * centred[None, :] * centred[None, :])
    )
    first, second = rotate(field[0], field[1], jnp.cos(phase), jnp.sin(phase), sign)
    return jnp.stack([first, second])


def propagate(field, delay, curv, sign):
    two, modes, length = field.shape
    parts = lax.axis_size("tm")
    block = length // parts
    total = length * parts
    mine = lax.axis_index("tm")
    rows = lax.all_to_all(field, "tm", split_axis=2, concat_axis=2, tiled=True)
    cos_first, sin_first = first_tables(mine, parts, block, total)
    rows = along_time(rows, cos_first, sin_first, -1.0, "ms,sk->mk")
    spectra = lax.all_to_all(rows, "tm", split_axis=2, concat_axis=2, tiled=True)
    cos_big, sin_big = tables(length, length, length)
    spectra = along_time(spectra, cos_big, sin_big, -1.0, "ms,sk->mk")
    local = jnp.arange(length, dtype=jnp.int32)
    ordered = lax.all_to_all(spectra, "tm", split_axis=2, concat_axis=2, tiled=True)
    freq = mine * length + local % block * parts + local // block
    ordered = apply_phase(ordered, freq, total, delay, curv, sign)
    spectra = lax.all_to_all(ordered, "tm", split_axis=2, concat_axis=2, tiled=True)
    spectra = along_time(spectra, cos_big, sin_big, 1.0, "ms,sk->mk")
    rows = lax.all_to_all(spectra, "tm", split_axis=2, concat_axis=2, tiled=True)
    rows = along_time(rows, cos_first, sin_first, 1.0, "mk,sk->ms") / total
    return lax.all_to_all(rows, "tm", split_axis=2, concat_axis=2, tiled=True)


def nonlinear(field, coupling):
    power = field[0] * field[0] + field[1] * field[1]
    angle = jnp.dot(coupling, power, precision=lax.Precision.HIGHEST)
    cosine = jnp.cos(angle)
    sine = jnp.sin(angle)
    return jnp.stack([field[0] * cosine - field[1] * sine, field[0] * sine + field[1] * cosine])


def kernel_of(taps):
    upper = jnp.concatenate([taps[0], -taps[1]], axis=1)
    lower = jnp.concatenate([taps[1], taps[0]], axis=1)
    return jnp.concatenate([upper, lower], axis=0)


def per_device(launch, target, taps, coupling, delay, curv):
    two, modes, length = launch.shape
    span = taps.shape[-1] - 1
    moved = propagate(launch, delay, curv, 1.0)
    mixed, nonlinear_pull = jax.vjp(lambda value: nonlinear(value, coupling), moved)
    history = passed_along(mixed[:, :, length - span :], "tm", 1)
    keeper = (lax.axis_index("tm") * length % WIN != 0).astype(jnp.float32)

    def apply_filter(before, own, coeffs):
        joined = jnp.concatenate([before * keeper, own], axis=2).reshape(
            1, two * modes, length + span
        )
        out = lax.conv_general_dilated(
            joined,
            kernel_of(coeffs),
            (1,),
            "VALID",
            dimension_numbers=("NCH", "OIH", "NCH"),
            precision=lax.Precision.HIGHEST,
        )
        return out.reshape(two, modes, length)

    output, filter_pull = jax.vjp(apply_filter, history, mixed, taps)
    misfit = output - target
    grad_before, grad_own, grad_coeffs = filter_pull(misfit)
    returned = passed_along(grad_before, "tm", -1)
    grad_own = grad_own + jnp.concatenate(
        [jnp.zeros((two, modes, length - span), jnp.float32), returned], axis=2
    )
    grad_moved = nonlinear_pull(grad_own)[0]
    launch_grad = propagate(grad_moved, delay, curv, -1.0)
    total = length * lax.axis_size("tm")
    tap_grad = lax.psum(grad_coeffs, "tm") / math.sqrt(total)
    return (misfit, launch_grad, tap_grad)


MESH = pl.DeviceIdType.MESH
LANES = 128
INNER = 8


def halves(table):
    high = table.astype(ml_dtypes.bfloat16)
    low = (table - high.astype(np.float64)).astype(ml_dtypes.bfloat16)
    return high, low


def dft_tables(parts, rows, held):
    count = parts * rows
    total = count * LANES
    k1 = np.arange(count)
    first = np.zeros((2, held, count, parts, held, 2, rows))
    t1 = (np.arange(parts)[:, None] * rows + np.arange(rows)[None, :])
    angle = 2.0 * np.pi * (k1[:, None, None] * t1[None] % count) / count
    wide = np.zeros((parts, held, 2, rows + 2, 2, held, count))
    t1w = np.arange(parts)[:, None] * rows + np.arange(rows + 2)[None, :] - 1
    inside = ((t1w >= 0) & (t1w < count)).astype(np.float64)
    anglew = 2.0 * np.pi * (t1w[:, :, None] * k1[None, None, :] % count) / count
    cosw, sinw = np.cos(anglew) * inside[:, :, None], np.sin(anglew) * inside[:, :, None]
    for m in range(held):
        first[0, m, :, :, m, 0, :] = np.cos(angle)
        first[0, m, :, :, m, 1, :] = np.sin(angle)
        first[1, m, :, :, m, 0, :] = -np.sin(angle)
        first[1, m, :, :, m, 1, :] = np.cos(angle)
        wide[:, m, 0, :, 0, m, :] = cosw
        wide[:, m, 0, :, 1, m, :] = -sinw
        wide[:, m, 1, :, 0, m, :] = sinw
        wide[:, m, 1, :, 1, m, :] = cosw
    size = 2 * held * count
    first = first.reshape(size, size)
    wide = wide.reshape(parts * held * 2 * (rows + 2), size)
    lane = np.arange(LANES)
    inner = 2.0 * np.pi * (lane[:, None] * lane[None, :] % LANES) / LANES
    cosine, sine = np.cos(inner), np.sin(inner)
    second = np.block([[cosine, -sine], [sine, cosine]])
    twist = 2.0 * np.pi * (k1[:, None] * lane[None, :]) / total
    freq = k1[:, None] + count * lane[None, :]
    centred = np.where(freq < total // 2, freq, freq - total) / total
    stack = lambda value: np.tile(value, (held, 1)).astype(np.float32)
    big = []
    for table in (first, first.T, wide, second, second.T):
        big += list(halves(np.ascontiguousarray(table)))
    return tuple(big) + (stack(np.cos(twist)), stack(np.sin(twist)), stack(centred))


def split(value):
    high = value.astype(jnp.bfloat16)
    return high, (value - high.astype(jnp.float32)).astype(jnp.bfloat16)


def dot3(left, right, dims=(((1,), (0,)), ((), ()))):
    one = functools.partial(lax.dot_general, dimension_numbers=dims, preferred_element_type=jnp.float32)
    return one(left[0], right[0]) + (one(left[0], right[1]) + one(left[1], right[0]))


SIN = [(-1) ** i * (2.0 * math.pi) ** (2 * i + 1) / math.factorial(2 * i + 1) for i in range(8)]
COS = [(-1) ** i * (2.0 * math.pi) ** (2 * i) / math.factorial(2 * i) for i in range(8)]


def circle(turns):
    quarter = jnp.round(turns * 4.0)
    rest = turns - quarter * 0.25
    square = rest * rest
    sine = jnp.full_like(rest, SIN[5])
    cosine = jnp.full_like(rest, COS[6])
    for i in range(4, -1, -1):
        sine = sine * square + SIN[i]
    for i in range(5, -1, -1):
        cosine = cosine * square + COS[i]
    sine = sine * rest
    which = quarter - 4.0 * jnp.floor(quarter * 0.25)
    odd = (which == 1.0) | (which == 3.0)
    cos_sign = jnp.where((which == 1.0) | (which == 2.0), -1.0, 1.0)
    sin_sign = jnp.where(which >= 2.0, -1.0, 1.0)
    return jnp.where(odd, sine, cosine) * cos_sign, jnp.where(odd, cosine, sine) * sin_sign


def kernel(
    parts, launch, target, a_in, b_in, coupling, coupling_t, delay, curv,
    f_h, f_l, ft_h, ft_l, wd_h, wd_l, s_h, s_l, st_h, st_l, tw_c, tw_s, grid_q,
    misfit_out, grad_out, tap_out,
    send1, recv1, send2, recv2, send3, recv3, send4, recv4, edge_send, edge, taps_own, rs1, half, rs2, mine_sum, gathered,
    a_h, a_l, b_h, b_l, x_h, x_l, prod, mc_h, mc_l, y_h, y_l,
    s_sem, r_sem, es_sem, er_sem, c_ssem, c_rsem,
):
    two, modes, length = launch.shape
    rows = length // LANES
    wide = rows + 2
    held = modes // parts
    count = parts * rows
    me = lax.axis_index("tm")
    chips = parts // 2
    chip, core = me // 2, me % 2
    sibling = chip * 2 + (1 - core)

    def at(index):
        return {"tm": index}

    def remote(source, dest, ssem, rsem, device):
        return pltpu.make_async_remote_copy(
            src_ref=source, dst_ref=dest, send_sem=ssem, recv_sem=rsem, device_id=at(device), device_id_type=MESH
        )

    def rows_of(ref, index, size):
        return ref.at[pl.ds(pl.multiple_of(index * size, 8), size), :]

    def exchange(phase, source, dest, size):
        def go(k, carry):
            other = lax.rem(me + k, parts)
            remote(rows_of(source, other, size), rows_of(dest, me, size), s_sem.at[phase, other], r_sem.at[phase, me], other).start()
            return carry

        lax.fori_loop(1, parts, go, 0)
        own = pl.ds(pl.multiple_of(me * size, 8), size)
        dest[own, :] = source[own, :]

    def arrive(phase, source, dest, size):
        def go(k, carry):
            other = lax.rem(me + parts - k, parts)
            remote(rows_of(source, other, size), rows_of(dest, other, size), s_sem.at[phase, other], r_sem.at[phase, other], other).wait_recv()
            return carry

        lax.fori_loop(1, parts, go, 0)

    def sent(phase, source, dest, size):
        def go(k, carry):
            other = lax.rem(me + k, parts)
            remote(rows_of(source, other, size), rows_of(dest, other, size), s_sem.at[phase, other], r_sem.at[phase, other], other).wait_send()
            return carry

        lax.fori_loop(1, parts, go, 0)

    barrier = pltpu.get_barrier_semaphore()

    def greet(k, carry):
        pl.semaphore_signal(barrier, inc=1, device_id=at(lax.rem(me + k, parts)), device_id_type=MESH)
        return carry

    lax.fori_loop(1, parts, greet, 0)
    for c in range(2):
        for r in range(rows):
            send1[pl.ds(c * rows + r, modes, stride=2 * rows), :] = launch[c, :, r * LANES : (r + 1) * LANES]
        edge_send[c * modes : (c + 1) * modes, :] = target[c, :, :LANES]
    pl.semaphore_wait(barrier, parts - 1)

    block = 2 * held * rows
    block_wide = 2 * held * wide
    exchange(0, send1, recv1, block)
    before, after = lax.rem(me + parts - 1, parts), lax.rem(me + 1, parts)
    edge_copy = remote(edge_send, edge, es_sem, er_sem, before)
    edge_copy.start()

    band = lax.broadcasted_iota(jnp.int32, (held * count, LANES), 0) // count
    q = grid_q[...]
    slope = jnp.zeros((held * count, LANES), jnp.float32)
    bend = jnp.zeros((held * count, LANES), jnp.float32)
    for m in range(held):
        slope = jnp.where(band == m, delay[me * held + m], slope)
        bend = jnp.where(band == m, curv[me * held + m], bend)
    phase_c, phase_s = circle(slope * q + bend * q * q)
    scale = 1.0 / (count * LANES)
    phase_c = phase_c * scale
    phase_s = phase_s * scale
    for source, high, low in ((a_in, a_h, a_l), (b_in, b_h, b_l)):
        high[...], low[...] = split(source[...])
    tc, ts = tw_c[...], tw_s[...]
    half_rows = held * count

    def disperse(received, sign, back_h, back_l):
        y = dot3((f_h[...], f_l[...]), split(received[...]))
        yr, yi = y[:half_rows], y[half_rows:]
        y = jnp.concatenate([yr * tc + yi * ts, yi * tc - yr * ts], axis=1)
        z = dot3(split(y), (s_h[...], s_l[...]))
        zr, zi = z[:, :LANES], z[:, LANES:]
        z = jnp.concatenate([zr * phase_c - sign * (zi * phase_s), zi * phase_c + sign * (zr * phase_s)], axis=1)
        u = dot3(split(z), (st_h[...], st_l[...]))
        ur, ui = u[:, :LANES], u[:, LANES:]
        u = jnp.concatenate([ur * tc - ui * ts, ui * tc + ur * ts], axis=0)
        return dot3((back_h[...], back_l[...]), split(u))

    arrive(0, send1, recv1, block)
    send2[...] = disperse(recv1, 1.0, wd_h, wd_l)
    exchange(1, send2, recv2, block_wide)
    arrive(1, send2, recv2, block_wide)

    def lanes_of(ref, c, span):
        return jnp.concatenate([ref[pl.ds(c * span + r, modes, stride=2 * span), :] for r in range(span)], axis=1)

    vr, vi = lanes_of(recv2, 0, wide), lanes_of(recv2, 1, wide)
    angle = dot3(split(coupling[...]), split(vr * vr + vi * vi))
    cosine, sine = circle(angle * (0.5 / math.pi))
    w = (vr * cosine - vi * sine, vr * sine + vi * cosine)
    full = wide * LANES
    ext = (rows + 1) * LANES
    outer = a_in.shape[0] // (2 * modes)
    span = outer * INNER

    for c in range(2):
        for j in range(INNER):
            moved = pltpu.roll(w[c], full - (LANES - span + j), 1)[:, :ext]
            high, low = split(moved)
            place = (slice(j * modes, (j + 1) * modes), slice(c * ext, (c + 1) * ext))
            x_h[place] = high
            x_l[place] = low
    prod[...] = dot3((a_h[...], a_l[...]), (x_h[...], x_l[...]))
    yr = jnp.zeros((modes, ext), jnp.float32)
    yi = jnp.zeros((modes, ext), jnp.float32)
    for b in range(outer):
        base = b * 2 * modes
        rr = prod[base : base + modes, :ext] - prod[base + modes : base + 2 * modes, ext:]
        ri = prod[base : base + modes, ext:] + prod[base + modes : base + 2 * modes, :ext]
        yr = yr + pltpu.roll(rr, ext - (INNER * b + 1), 1)
        yi = yi + pltpu.roll(ri, ext - (INNER * b + 1), 1)
    remote(edge_send, edge, es_sem, er_sem, after).wait_recv()
    lane = lax.broadcasted_iota(jnp.int32, (modes, LANES), 1)
    keep = (lane < span) & (me != parts - 1)
    m = []
    for c, y in ((0, yr), (1, yi)):
        own = y[:, :length] - target[c]
        misfit_out[c] = own
        m.append((own, jnp.where(keep, y[:, length:] - edge[c * modes : (c + 1) * modes, :], 0.0)))

    zero = jnp.zeros((modes, LANES), jnp.float32)
    own = [jnp.concatenate([part[0], zero], axis=1) for part in m]
    for b in range(outer):
        base = b * 2 * modes
        first = split(pltpu.roll(own[0], INNER * b + 1, 1))
        second = split(pltpu.roll(own[1], INNER * b + 1, 1))
        for ref, one, two_ in ((mc_h, first[0], second[0]), (mc_l, first[1], second[1])):
            ref[base : base + modes, :ext] = one
            ref[base : base + modes, ext:] = two_
            ref[base + modes : base + 2 * modes, :ext] = two_
            ref[base + modes : base + 2 * modes, ext:] = -one
    taps_own[...] = dot3((mc_h[...], mc_l[...]), (x_h[...], x_l[...]), (((1,), (1,)), ((), ())))
    half_size = taps_own.shape[0] // 2
    piece = half_size // chips
    swap = remote(rows_of(taps_own, 1 - core, half_size), rs1, c_ssem.at[0], c_rsem.at[0], sibling)
    swap.start()

    joined = [jnp.concatenate(part, axis=1) for part in m]
    for c in range(2):
        for j in range(INNER):
            moved = joined[c] if j == INNER - 1 else pltpu.roll(joined[c], ext - (INNER - 1 - j), 1)
            high, low = split(moved)
            place = (slice(j * modes, (j + 1) * modes), slice(c * ext, (c + 1) * ext))
            y_h[place] = high
            y_l[place] = low
    prod[...] = dot3((b_h[...], b_l[...]), (y_h[...], y_l[...]))

    swap.wait_recv()
    half[...] = taps_own[pl.ds(pl.multiple_of(core * half_size, 8), half_size), :] + rs1[...]

    def scatter(k, carry):
        other = lax.rem(chip + k, chips)
        remote(rows_of(half, other, piece), rows_of(rs2, chip, piece), c_ssem.at[1 + other], c_rsem.at[1 + chip], other * 2 + core).start()
        return carry

    lax.fori_loop(1, chips, scatter, 0)

    gr = jnp.zeros((modes, length), jnp.float32)
    gi = jnp.zeros((modes, length), jnp.float32)
    for b in range(outer):
        base = b * 2 * modes
        rr = prod[base : base + modes, :ext] + prod[base + modes : base + 2 * modes, ext:]
        ri = prod[base : base + modes, ext:] - prod[base + modes : base + 2 * modes, :ext]
        shift = span - INNER - INNER * b
        if shift:
            rr = pltpu.roll(rr, ext - shift, 1)
            ri = pltpu.roll(ri, ext - shift, 1)
        gr = gr + rr[:, :length]
        gi = gi + ri[:, :length]
    here = slice(LANES, LANES + length)
    wr, wi, cosine, sine = w[0][:, here], w[1][:, here], cosine[:, here], sine[:, here]
    pull = dot3(split(coupling_t[...]), split(gi * wr - gr * wi)) * 2.0
    vr = gr * cosine + gi * sine + vr[:, here] * pull
    vi = gi * cosine - gr * sine + vi[:, here] * pull
    for c, value in ((0, vr), (1, vi)):
        for r in range(rows):
            send3[pl.ds(c * rows + r, modes, stride=2 * rows), :] = value[:, r * LANES : (r + 1) * LANES]
    exchange(2, send3, recv3, block)
    arrive(2, send3, recv3, block)
    send4[...] = disperse(recv3, -1.0, ft_h, ft_l)
    exchange(3, send4, recv4, block)

    def scattered(k, carry):
        other = lax.rem(chip + chips - k, chips)
        remote(rows_of(half, other, piece), rows_of(rs2, other, piece), c_ssem.at[1 + other], c_rsem.at[1 + other], other * 2 + core).wait_recv()
        return carry

    lax.fori_loop(1, chips, scattered, 0)
    own_piece = pl.ds(pl.multiple_of(chip * piece, 8), piece)
    rs2[own_piece, :] = half[own_piece, :]
    total = rs2[:piece, :]
    for k in range(1, chips):
        total = total + rs2[k * piece : (k + 1) * piece, :]
    mine_sum[...] = total * (1.0 / math.sqrt(count * LANES))
    base = 1 + chips

    def slot(c_, k_):
        return rows_of(gathered, c_ * chips + k_, piece)

    def spread(k, carry):
        other = lax.rem(chip + k, chips)
        remote(mine_sum, slot(core, chip), c_ssem.at[base + other], c_rsem.at[base + chip], other * 2 + core).start()
        return carry

    lax.fori_loop(1, chips, spread, 0)
    base2 = base + chips
    remote(mine_sum, slot(core, chip), c_ssem.at[base2 + chip], c_rsem.at[base2 + chip], sibling).start()
    gathered[pl.ds(pl.multiple_of((core * chips + chip) * piece, 8), piece), :] = mine_sum[...]

    arrive(3, send4, recv4, block)
    for c in range(2):
        grad_out[c] = lanes_of(recv4, c, rows)

    def pass_on(k, carry):
        other = lax.rem(chip + chips - k, chips)
        remote(mine_sum, slot(core, other), c_ssem.at[base + other], c_rsem.at[base + other], other * 2 + core).wait_recv()
        remote(slot(core, other), slot(core, other), c_ssem.at[base2 + other], c_rsem.at[base2 + other], sibling).start()
        return carry

    lax.fori_loop(1, chips, pass_on, 0)

    def collect(k, carry):
        other = lax.rem(chip + chips - k, chips)
        remote(slot(1 - core, other), slot(1 - core, other), c_ssem.at[base2 + other], c_rsem.at[base2 + other], sibling).wait_recv()
        return carry

    lax.fori_loop(0, chips, collect, 0)
    tap_out[...] = gathered[...]

    edge_copy.wait_send()
    swap.wait_send()
    sent(0, send1, recv1, block)
    sent(1, send2, recv2, block_wide)
    sent(2, send3, recv3, block)
    sent(3, send4, recv4, block)

    def left(k, carry):
        other = lax.rem(chip + k, chips)
        remote(rows_of(half, other, piece), rows_of(rs2, other, piece), c_ssem.at[1 + other], c_rsem.at[1 + other], sibling).wait_send()
        remote(mine_sum, slot(core, other), c_ssem.at[base + other], c_rsem.at[base + other], sibling).wait_send()
        return carry

    lax.fori_loop(1, chips, left, 0)

    def handed(k, carry):
        other = lax.rem(chip + chips - k, chips)
        remote(slot(core, other), slot(core, other), c_ssem.at[base2 + other], c_rsem.at[base2 + other], sibling).wait_send()
        return carry

    lax.fori_loop(1, chips, handed, 0)
    remote(mine_sum, slot(core, chip), c_ssem.at[base2 + chip], c_rsem.at[base2 + chip], sibling).wait_send()


def fused(launch, target, taps, coupling, delay, curv):
    two, modes, length = launch.shape
    parts = lax.axis_size("tm")
    span = taps.shape[-1]
    outer = span // INNER
    rows = length // LANES
    held = modes // parts
    wide = (rows + 2) * parts * held * 2
    plain = rows * parts * held * 2
    ext = (rows + 1) * LANES
    chips = parts // 2
    pieces = taps.reshape(2, modes, modes, outer, INNER)
    forward = pieces.transpose(3, 0, 1, 4, 2).reshape(outer * 2 * modes, INNER * modes)
    backward = pieces.transpose(3, 0, 2, 4, 1).reshape(outer * 2 * modes, INNER * modes)
    size = outer * 2 * modes
    cols = INNER * modes
    tables_ = [jnp.asarray(table) for table in dft_tables(parts, rows, held)]
    vmem = pl.BlockSpec(memory_space=pltpu.VMEM)
    smem = pl.BlockSpec(memory_space=pltpu.SMEM)
    f32, bf16 = jnp.float32, jnp.bfloat16
    field = lambda n: pltpu.VMEM((n, LANES), f32)
    misfit, launch_grad, tap = pl.pallas_call(
        functools.partial(kernel, parts),
        out_shape=(
            jax.ShapeDtypeStruct((2, modes, length), f32),
            jax.ShapeDtypeStruct((2, modes, length), f32),
            jax.ShapeDtypeStruct((size, cols), f32),
        ),
        in_specs=[vmem] * 6 + [smem] * 2 + [vmem] * len(tables_),
        out_specs=(vmem, vmem, vmem),
        scratch_shapes=[
            field(plain), field(plain), field(wide), field(wide), field(plain), field(plain), field(plain), field(plain),
            field(2 * modes), field(2 * modes),
            pltpu.VMEM((size, cols), f32), pltpu.VMEM((size // 2, cols), f32), pltpu.VMEM((size // 2, cols), f32),
            pltpu.VMEM((size // 2, cols), f32), pltpu.VMEM((size // parts, cols), f32), pltpu.VMEM((size, cols), f32),
            pltpu.VMEM((size, cols), bf16), pltpu.VMEM((size, cols), bf16),
            pltpu.VMEM((size, cols), bf16), pltpu.VMEM((size, cols), bf16),
            pltpu.VMEM((cols, 2 * ext), bf16), pltpu.VMEM((cols, 2 * ext), bf16),
            pltpu.VMEM((size, 2 * ext), f32),
            pltpu.VMEM((size, 2 * ext), bf16), pltpu.VMEM((size, 2 * ext), bf16),
            pltpu.VMEM((cols, 2 * ext), bf16), pltpu.VMEM((cols, 2 * ext), bf16),
            pltpu.SemaphoreType.DMA((4, parts)), pltpu.SemaphoreType.DMA((4, parts)),
            pltpu.SemaphoreType.DMA, pltpu.SemaphoreType.DMA,
            pltpu.SemaphoreType.DMA((1 + 3 * chips,)), pltpu.SemaphoreType.DMA((1 + 3 * chips,)),
        ],
        compiler_params=pltpu.CompilerParams(collective_id=0, has_side_effects=True, vmem_limit_bytes=48 * 1024 * 1024),
    )(launch, target, forward, backward, coupling, coupling.T, delay, curv, *tables_)
    tap = tap.reshape(outer, 2, modes, INNER, modes).transpose(1, 2, 4, 0, 3).reshape(taps.shape)
    return misfit, launch_grad, tap


def fits(launch, taps, parts):
    two, modes, length = launch.shape
    return (
        parts % 2 == 0
        and parts > 2
        and modes % parts == 0
        and modes % 16 == 0
        and length % LANES == 0
        and length * parts == WIN
        and taps.shape[-1] % INNER == 0
        and taps.shape[-1] < LANES
        and (2 * (modes // parts) * (length // LANES)) % 8 == 0
        and (2 * (modes // parts) * (length // LANES + 2)) % 8 == 0
    )


def choose(launch, target, taps, coupling, delay, curv):
    if fits(launch, taps, lax.axis_size("tm")):
        return fused(launch, target, taps, coupling, delay, curv)
    return per_device(launch, target, taps, coupling, delay, curv)


def solution(mesh):
    in_specs = (P(None, None, ("grp", "tm")), P(None, None, ("grp", "tm")), P(), P(), P(), P())
    out_specs = (
        P(None, None, ("grp", "tm")),
        P(None, None, ("grp", "tm")),
        P("grp", None, None, None),
    )
    return jax.shard_map(
        choose, mesh=mesh, in_specs=in_specs, out_specs=out_specs, check_vma=False
    )
```

```python
import functools
import math

import jax
import jax.numpy as jnp
import ml_dtypes
import numpy as np
from jax import lax
from jax.experimental import pallas as pl
from jax.experimental.pallas import tpu as pltpu
from jax.sharding import PartitionSpec as P


WIN = 8192


def passed_along(block, axis, distance):
    devices = range(lax.axis_size(axis))
    route = [(i - distance, i) for i in devices if i - distance in devices]
    return lax.ppermute(block, axis, route)


def tables(rows, cols, modulus):
    left = jnp.arange(rows, dtype=jnp.int32)[:, None]
    right = jnp.arange(cols, dtype=jnp.int32)[None, :]
    angle = (left * right % modulus).astype(jnp.float32) * (2.0 * math.pi / modulus)
    return (jnp.cos(angle), jnp.sin(angle))


def first_tables(mine, parts, block, total):
    length = parts * block
    index = jnp.arange(length, dtype=jnp.int32)
    outer = index // block
    inner = index % block
    sample = outer[:, None] * length + mine * block + inner[:, None]
    angle = (outer[None, :] * sample % total).astype(jnp.float32) * (2.0 * math.pi / total)
    same = (inner[:, None] == inner[None, :]).astype(jnp.float32)
    return (jnp.cos(angle) * same, jnp.sin(angle) * same)


def rotate(real_part, imag_part, cosine, sine, sign):
    return (
        real_part * cosine - sign * imag_part * sine,
        imag_part * cosine + sign * real_part * sine,
    )


def along_time(field, cosine, sine, sign, form):
    high = lax.Precision.HIGHEST
    cos_real = jnp.einsum(form, field[0], cosine, precision=high)
    cos_imag = jnp.einsum(form, field[1], cosine, precision=high)
    sin_real = jnp.einsum(form, field[0], sine, precision=high)
    sin_imag = jnp.einsum(form, field[1], sine, precision=high)
    return jnp.stack([cos_real - sign * sin_imag, cos_imag + sign * sin_real])


def apply_phase(field, freq, total, delay, curv, sign):
    centred = jnp.where(freq < total // 2, freq, freq - total).astype(jnp.float32) / total
    phase = (
        2.0
        * math.pi
        * (delay[:, None] * centred[None, :] + curv[:, None] * centred[None, :] * centred[None, :])
    )
    first, second = rotate(field[0], field[1], jnp.cos(phase), jnp.sin(phase), sign)
    return jnp.stack([first, second])


def propagate(field, delay, curv, sign):
    two, modes, length = field.shape
    parts = lax.axis_size("tm")
    block = length // parts
    total = length * parts
    mine = lax.axis_index("tm")
    rows = lax.all_to_all(field, "tm", split_axis=2, concat_axis=2, tiled=True)
    cos_first, sin_first = first_tables(mine, parts, block, total)
    rows = along_time(rows, cos_first, sin_first, -1.0, "ms,sk->mk")
    spectra = lax.all_to_all(rows, "tm", split_axis=2, concat_axis=2, tiled=True)
    cos_big, sin_big = tables(length, length, length)
    spectra = along_time(spectra, cos_big, sin_big, -1.0, "ms,sk->mk")
    local = jnp.arange(length, dtype=jnp.int32)
    ordered = lax.all_to_all(spectra, "tm", split_axis=2, concat_axis=2, tiled=True)
    freq = mine * length + local % block * parts + local // block
    ordered = apply_phase(ordered, freq, total, delay, curv, sign)
    spectra = lax.all_to_all(ordered, "tm", split_axis=2, concat_axis=2, tiled=True)
    spectra = along_time(spectra, cos_big, sin_big, 1.0, "ms,sk->mk")
    rows = lax.all_to_all(spectra, "tm", split_axis=2, concat_axis=2, tiled=True)
    rows = along_time(rows, cos_first, sin_first, 1.0, "mk,sk->ms") / total
    return lax.all_to_all(rows, "tm", split_axis=2, concat_axis=2, tiled=True)


def nonlinear(field, coupling):
    power = field[0] * field[0] + field[1] * field[1]
    angle = jnp.dot(coupling, power, precision=lax.Precision.HIGHEST)
    cosine = jnp.cos(angle)
    sine = jnp.sin(angle)
    return jnp.stack([field[0] * cosine - field[1] * sine, field[0] * sine + field[1] * cosine])


def kernel_of(taps):
    upper = jnp.concatenate([taps[0], -taps[1]], axis=1)
    lower = jnp.concatenate([taps[1], taps[0]], axis=1)
    return jnp.concatenate([upper, lower], axis=0)


def per_device(launch, target, taps, coupling, delay, curv):
    two, modes, length = launch.shape
    span = taps.shape[-1] - 1
    moved = propagate(launch, delay, curv, 1.0)
    mixed, nonlinear_pull = jax.vjp(lambda value: nonlinear(value, coupling), moved)
    history = passed_along(mixed[:, :, length - span :], "tm", 1)
    keeper = (lax.axis_index("tm") * length % WIN != 0).astype(jnp.float32)

    def apply_filter(before, own, coeffs):
        joined = jnp.concatenate([before * keeper, own], axis=2).reshape(
            1, two * modes, length + span
        )
        out = lax.conv_general_dilated(
            joined,
            kernel_of(coeffs),
            (1,),
            "VALID",
            dimension_numbers=("NCH", "OIH", "NCH"),
            precision=lax.Precision.HIGHEST,
        )
        return out.reshape(two, modes, length)

    output, filter_pull = jax.vjp(apply_filter, history, mixed, taps)
    misfit = output - target
    grad_before, grad_own, grad_coeffs = filter_pull(misfit)
    returned = passed_along(grad_before, "tm", -1)
    grad_own = grad_own + jnp.concatenate(
        [jnp.zeros((two, modes, length - span), jnp.float32), returned], axis=2
    )
    grad_moved = nonlinear_pull(grad_own)[0]
    launch_grad = propagate(grad_moved, delay, curv, -1.0)
    total = length * lax.axis_size("tm")
    tap_grad = lax.psum(grad_coeffs, "tm") / math.sqrt(total)
    return (misfit, launch_grad, tap_grad)


MESH = pl.DeviceIdType.MESH
LANES = 128
INNER = 8
TABLES = 13


def halves(table):
    high = table.astype(ml_dtypes.bfloat16)
    low = (table - high.astype(np.float64)).astype(ml_dtypes.bfloat16)
    return high, low


def dft_tables(parts, rows, held):
    count = parts * rows
    total = count * LANES
    k1 = np.arange(count)
    first = np.zeros((2, held, count, parts, held, 2, rows))
    t1 = (np.arange(parts)[:, None] * rows + np.arange(rows)[None, :])
    angle = 2.0 * np.pi * (k1[:, None, None] * t1[None] % count) / count
    wide = np.zeros((parts, held, 2, rows + 2, 2, held, count))
    t1w = np.arange(parts)[:, None] * rows + np.arange(rows + 2)[None, :] - 1
    inside = ((t1w >= 0) & (t1w < count)).astype(np.float64)
    anglew = 2.0 * np.pi * (t1w[:, :, None] * k1[None, None, :] % count) / count
    cosw, sinw = np.cos(anglew) * inside[:, :, None], np.sin(anglew) * inside[:, :, None]
    for m in range(held):
        first[0, m, :, :, m, 0, :] = np.cos(angle)
        first[0, m, :, :, m, 1, :] = np.sin(angle)
        first[1, m, :, :, m, 0, :] = -np.sin(angle)
        first[1, m, :, :, m, 1, :] = np.cos(angle)
        wide[:, m, 0, :, 0, m, :] = cosw
        wide[:, m, 0, :, 1, m, :] = -sinw
        wide[:, m, 1, :, 0, m, :] = sinw
        wide[:, m, 1, :, 1, m, :] = cosw
    size = 2 * held * count
    first = first.reshape(size, size)
    wide = wide.reshape(parts * held * 2 * (rows + 2), size)
    lane = np.arange(LANES)
    inner = 2.0 * np.pi * (lane[:, None] * lane[None, :] % LANES) / LANES
    cosine, sine = np.cos(inner), np.sin(inner)
    second = np.block([[cosine, -sine], [sine, cosine]])
    twist = 2.0 * np.pi * (k1[:, None] * lane[None, :]) / total
    freq = k1[:, None] + count * lane[None, :]
    centred = np.where(freq < total // 2, freq, freq - total) / total
    stack = lambda value: np.tile(value, (held, 1)).astype(np.float32)
    big = []
    for table in (first, first.T, wide, second, second.T):
        big += list(halves(np.ascontiguousarray(table)))
    return tuple(big) + (stack(np.cos(twist)), stack(np.sin(twist)), stack(centred))


def split(value):
    high = value.astype(jnp.bfloat16)
    return high, (value - high.astype(jnp.float32)).astype(jnp.bfloat16)


def dot3(left, right, dims=(((1,), (0,)), ((), ()))):
    one = functools.partial(lax.dot_general, dimension_numbers=dims, preferred_element_type=jnp.float32)
    return one(left[0], right[0]) + (one(left[0], right[1]) + one(left[1], right[0]))


SIN = [(-1) ** i * (2.0 * math.pi) ** (2 * i + 1) / math.factorial(2 * i + 1) for i in range(8)]
COS = [(-1) ** i * (2.0 * math.pi) ** (2 * i) / math.factorial(2 * i) for i in range(8)]


def circle(turns):
    quarter = jnp.round(turns * 4.0)
    rest = turns - quarter * 0.25
    square = rest * rest
    sine = jnp.full_like(rest, SIN[5])
    cosine = jnp.full_like(rest, COS[6])
    for i in range(4, -1, -1):
        sine = sine * square + SIN[i]
    for i in range(5, -1, -1):
        cosine = cosine * square + COS[i]
    sine = sine * rest
    which = quarter - 4.0 * jnp.floor(quarter * 0.25)
    odd = (which == 1.0) | (which == 3.0)
    cos_sign = jnp.where((which == 1.0) | (which == 2.0), -1.0, 1.0)
    sin_sign = jnp.where(which >= 2.0, -1.0, 1.0)
    return jnp.where(odd, sine, cosine) * cos_sign, jnp.where(odd, cosine, sine) * sin_sign


def kernel(
    parts, launch, target, coupling, delay, curv, taps_far, *rest,
):
    far, rest = rest[:TABLES], rest[TABLES:]
    misfit_out, grad_out, tap_out = rest[:3]
    taps_in, *near = rest[3 : 4 + TABLES]
    (f_h, f_l, ft_h, ft_l, wd_h, wd_l, s_h, s_l, st_h, st_l, tw_c, tw_s, grid_q) = near
    (
    send1, recv1, send2, recv2, send3, recv3, send4, recv4, edge_send, edge, taps_own, rs1, half, rs2, mine_sum, gathered,
    turned, a_f, a_h, a_l, b_h, b_l, x_h, x_l, prod, mc_h, mc_l, grad_w,
    s_sem, r_sem, es_sem, er_sem, c_ssem, c_rsem, l_sem,
    ) = rest[4 + TABLES :]
    two, modes, length = launch.shape
    rows = length // LANES
    wide = rows + 2
    held = modes // parts
    count = parts * rows
    me = lax.axis_index("tm")
    chips = parts // 2
    chip, core = me // 2, me % 2
    sibling = chip * 2 + (1 - core)

    def at(index):
        return {"tm": index}

    def remote(source, dest, ssem, rsem, device):
        return pltpu.make_async_remote_copy(
            src_ref=source, dst_ref=dest, send_sem=ssem, recv_sem=rsem, device_id=at(device), device_id_type=MESH
        )

    def rows_of(ref, index, size):
        return ref.at[pl.ds(pl.multiple_of(index * size, 8), size), :]

    def exchange(phase, source, dest, size):
        def go(k, carry):
            other = lax.rem(me + k, parts)
            remote(rows_of(source, other, size), rows_of(dest, me, size), s_sem.at[phase, other], r_sem.at[phase, me], other).start()
            return carry

        lax.fori_loop(1, parts, go, 0)
        own = pl.ds(pl.multiple_of(me * size, 8), size)
        dest[own, :] = source[own, :]

    def arrive(phase, source, dest, size):
        def go(k, carry):
            other = lax.rem(me + parts - k, parts)
            remote(rows_of(source, other, size), rows_of(dest, other, size), s_sem.at[phase, other], r_sem.at[phase, other], other).wait_recv()
            return carry

        lax.fori_loop(1, parts, go, 0)

    def sent(phase, source, dest, size):
        def go(k, carry):
            other = lax.rem(me + k, parts)
            remote(rows_of(source, other, size), rows_of(dest, other, size), s_sem.at[phase, other], r_sem.at[phase, other], other).wait_send()
            return carry

        lax.fori_loop(1, parts, go, 0)

    loads = [pltpu.make_async_copy(taps_far, taps_in, l_sem.at[0])]
    loads += [pltpu.make_async_copy(one, two_, l_sem.at[1 + i]) for i, (one, two_) in enumerate(zip(far, near))]
    for load in loads:
        load.start()
    barrier = pltpu.get_barrier_semaphore()

    def greet(k, carry):
        pl.semaphore_signal(barrier, inc=1, device_id=at(lax.rem(me + k, parts)), device_id_type=MESH)
        return carry

    lax.fori_loop(1, parts, greet, 0)
    for c in range(2):
        for r in range(rows):
            send1[pl.ds(c * rows + r, modes, stride=2 * rows), :] = launch[c, :, r * LANES : (r + 1) * LANES]
        edge_send[c * modes : (c + 1) * modes, :] = target[c, :, :LANES]
    pl.semaphore_wait(barrier, parts - 1)

    block = 2 * held * rows
    block_wide = 2 * held * wide
    exchange(0, send1, recv1, block)
    before, after = lax.rem(me + parts - 1, parts), lax.rem(me + 1, parts)
    edge_copy = remote(edge_send, edge, es_sem, er_sem, before)
    edge_copy.start()

    for load in loads:
        load.wait()
    band = lax.broadcasted_iota(jnp.int32, (held * count, LANES), 0) // count
    q = grid_q[...]
    slope = jnp.zeros((held * count, LANES), jnp.float32)
    bend = jnp.zeros((held * count, LANES), jnp.float32)
    for m in range(held):
        slope = jnp.where(band == m, delay[me * held + m], slope)
        bend = jnp.where(band == m, curv[me * held + m], bend)
    phase_c, phase_s = circle(slope * q + bend * q * q)
    scale = 1.0 / (count * LANES)
    phase_c = phase_c * scale
    phase_s = phase_s * scale
    outer = turned.shape[0] // INNER
    group = LANES // modes
    both = 2 * modes
    lane_group = lax.broadcasted_iota(jnp.int32, (outer, LANES), 1) // modes
    for tile in range(both // group):
        turned[...] = jnp.transpose(taps_in[tile * LANES : (tile + 1) * LANES, :])
        for h in range(INNER // group):
            lines = [turned[pl.ds(h * group + jj, outer, stride=INNER), :] for jj in range(group)]
            for o in range(group):
                value = None
                for jj in range(group):
                    turn = (jj - o) % group * modes
                    line = pltpu.roll(lines[jj], turn, 1) if turn else lines[jj]
                    value = line if value is None else jnp.where(lane_group == jj, line, value)
                at_row = h * both * outer + (tile * group + o) * outer
                a_f[at_row : at_row + outer, :] = value
    tile_count = INNER // group
    lines = []
    for b in range(outer):
        strips = [a_f[pl.ds(h * both * outer + b, both, stride=outer), :] for h in range(tile_count)]
        lines.append(jnp.concatenate(strips, axis=1))
        place = slice(b * both, (b + 1) * both)
        a_h[place, :], a_l[place, :] = split(lines[-1])
    b_h[...], b_l[...] = split(jnp.transpose(jnp.concatenate(lines, axis=0)))
    tc, ts = tw_c[...], tw_s[...]
    half_rows = held * count

    def disperse(received, sign, back_h, back_l):
        y = dot3((f_h[...], f_l[...]), split(received[...]))
        yr, yi = y[:half_rows], y[half_rows:]
        y = jnp.concatenate([yr * tc + yi * ts, yi * tc - yr * ts], axis=1)
        z = dot3(split(y), (s_h[...], s_l[...]))
        zr, zi = z[:, :LANES], z[:, LANES:]
        z = jnp.concatenate([zr * phase_c - sign * (zi * phase_s), zi * phase_c + sign * (zr * phase_s)], axis=1)
        u = dot3(split(z), (st_h[...], st_l[...]))
        ur, ui = u[:, :LANES], u[:, LANES:]
        u = jnp.concatenate([ur * tc - ui * ts, ui * tc + ur * ts], axis=0)
        return dot3((back_h[...], back_l[...]), split(u))

    arrive(0, send1, recv1, block)
    send2[...] = disperse(recv1, 1.0, wd_h, wd_l)
    exchange(1, send2, recv2, block_wide)
    arrive(1, send2, recv2, block_wide)

    def lanes_of(ref, c, span):
        return jnp.concatenate([ref[pl.ds(c * span + r, modes, stride=2 * span), :] for r in range(span)], axis=1)

    vr, vi = lanes_of(recv2, 0, wide), lanes_of(recv2, 1, wide)
    angle = dot3(split(coupling[...]), split(vr * vr + vi * vi))
    cosine, sine = circle(angle * (0.5 / math.pi))
    w = (vr * cosine - vi * sine, vr * sine + vi * cosine)
    full = wide * LANES
    ext = (rows + 1) * LANES
    span = outer * INNER

    for c in range(2):
        for j in range(INNER):
            moved = pltpu.roll(w[c], full - (LANES - span + j), 1)[:, :ext]
            high, low = split(moved)
            place = (slice(j * modes, (j + 1) * modes), slice(c * ext, (c + 1) * ext))
            x_h[place] = high
            x_l[place] = low
    prod[...] = dot3((a_h[...], a_l[...]), (x_h[...], x_l[...]))
    yr = jnp.zeros((modes, ext), jnp.float32)
    yi = jnp.zeros((modes, ext), jnp.float32)
    for b in range(outer):
        base = b * 2 * modes
        rr = prod[base : base + modes, :ext] - prod[base + modes : base + 2 * modes, ext:]
        ri = prod[base : base + modes, ext:] + prod[base + modes : base + 2 * modes, :ext]
        yr = yr + pltpu.roll(rr, ext - (INNER * b + 1), 1)
        yi = yi + pltpu.roll(ri, ext - (INNER * b + 1), 1)
    remote(edge_send, edge, es_sem, er_sem, after).wait_recv()
    lane = lax.broadcasted_iota(jnp.int32, (modes, LANES), 1)
    keep = (lane < span) & (me != parts - 1)
    m = []
    for c, y in ((0, yr), (1, yi)):
        own = y[:, :length] - target[c]
        misfit_out[c] = own
        m.append((own, jnp.where(keep, y[:, length:] - edge[c * modes : (c + 1) * modes, :], 0.0)))

    m = [jnp.concatenate(part, axis=1) for part in m]
    for b in range(outer):
        base = b * 2 * modes
        first = split(pltpu.roll(m[0], INNER * b + 1, 1))
        second = split(pltpu.roll(m[1], INNER * b + 1, 1))
        for ref, one, two_ in ((mc_h, first[0], second[0]), (mc_l, first[1], second[1])):
            ref[base : base + modes, :ext] = one
            ref[base : base + modes, ext:] = two_
            ref[base + modes : base + 2 * modes, :ext] = two_
            ref[base + modes : base + 2 * modes, ext:] = -one
    for start in (0, length, ext, ext + length):
        shift = lax.broadcasted_iota(jnp.int32, (INNER * modes, LANES), 0) // modes
        sample = lax.broadcasted_iota(jnp.int32, (INNER * modes, LANES), 1) + shift + (start % ext - span)
        inside = (sample >= 0) & (sample < length)
        for ref in (x_h, x_l):
            strip = ref[:, start : start + LANES].astype(jnp.float32)
            ref[:, start : start + LANES] = jnp.where(inside, strip, 0.0).astype(jnp.bfloat16)
    coeffs = dot3((mc_h[...], mc_l[...]), (x_h[...], x_l[...]), (((1,), (1,)), ((), ())))
    for b in range(outer):
        for h in range(tile_count):
            a_f[pl.ds(h * both * outer + b, both, stride=outer), :] = coeffs[b * both : (b + 1) * both, h * LANES : (h + 1) * LANES]
    for h in range(tile_count):
        taps_own[:, h * LANES : (h + 1) * LANES] = a_f[h * both * outer : (h + 1) * both * outer, :]
    half_size = taps_own.shape[0] // 2
    piece = half_size // chips
    swap = remote(rows_of(taps_own, 1 - core, half_size), rs1, c_ssem.at[0], c_rsem.at[0], sibling)
    swap.start()

    grad_w[...] = dot3((b_h[...], b_l[...]), (mc_h[...], mc_l[...]))

    swap.wait_recv()
    half[...] = taps_own[pl.ds(pl.multiple_of(core * half_size, 8), half_size), :] + rs1[...]

    def scatter(k, carry):
        other = lax.rem(chip + k, chips)
        remote(rows_of(half, other, piece), rows_of(rs2, chip, piece), c_ssem.at[1 + other], c_rsem.at[1 + chip], other * 2 + core).start()
        return carry

    lax.fori_loop(1, chips, scatter, 0)

    gr = jnp.zeros((modes, length), jnp.float32)
    gi = jnp.zeros((modes, length), jnp.float32)
    for j in range(INNER):
        rows_j = slice(j * modes, (j + 1) * modes)
        gr = gr + pltpu.roll(grad_w[rows_j, :ext], ext - (span - j), 1)[:, :length]
        gi = gi + pltpu.roll(grad_w[rows_j, ext:], ext - (span - j), 1)[:, :length]
    here = slice(LANES, LANES + length)
    wr, wi, cosine, sine = w[0][:, here], w[1][:, here], cosine[:, here], sine[:, here]
    pull = dot3(split(jnp.transpose(coupling[...])), split(gi * wr - gr * wi)) * 2.0
    vr = gr * cosine + gi * sine + vr[:, here] * pull
    vi = gi * cosine - gr * sine + vi[:, here] * pull
    for c, value in ((0, vr), (1, vi)):
        for r in range(rows):
            send3[pl.ds(c * rows + r, modes, stride=2 * rows), :] = value[:, r * LANES : (r + 1) * LANES]
    exchange(2, send3, recv3, block)
    arrive(2, send3, recv3, block)
    send4[...] = disperse(recv3, -1.0, ft_h, ft_l)
    exchange(3, send4, recv4, block)

    def scattered(k, carry):
        other = lax.rem(chip + chips - k, chips)
        remote(rows_of(half, other, piece), rows_of(rs2, other, piece), c_ssem.at[1 + other], c_rsem.at[1 + other], other * 2 + core).wait_recv()
        return carry

    lax.fori_loop(1, chips, scattered, 0)
    own_piece = pl.ds(pl.multiple_of(chip * piece, 8), piece)
    rs2[own_piece, :] = half[own_piece, :]
    total = rs2[:piece, :]
    for k in range(1, chips):
        total = total + rs2[k * piece : (k + 1) * piece, :]
    total = total * (1.0 / math.sqrt(count * LANES))
    for h in range(INNER // group):
        for jj in range(group):
            value = None
            for o in range(group):
                turn = (o - jj) % group * modes
                line = total[o * outer : (o + 1) * outer, h * LANES : (h + 1) * LANES]
                line = pltpu.roll(line, turn, 1) if turn else line
                value = line if value is None else jnp.where(lane_group == o, line, value)
            mine_sum[pl.ds(h * group + jj, outer, stride=INNER), :] = value
    base = 1 + chips

    def slot(c_, k_):
        return rows_of(gathered, c_ * chips + k_, span)

    def spread(k, carry):
        other = lax.rem(chip + k, chips)
        remote(mine_sum, slot(core, chip), c_ssem.at[base + other], c_rsem.at[base + chip], other * 2 + core).start()
        return carry

    lax.fori_loop(1, chips, spread, 0)
    base2 = base + chips
    remote(mine_sum, slot(core, chip), c_ssem.at[base2 + chip], c_rsem.at[base2 + chip], sibling).start()
    gathered[pl.ds(pl.multiple_of((core * chips + chip) * span, 8), span), :] = mine_sum[...]

    arrive(3, send4, recv4, block)
    for c in range(2):
        grad_out[c] = lanes_of(recv4, c, rows)

    def pass_on(k, carry):
        other = lax.rem(chip + chips - k, chips)
        remote(mine_sum, slot(core, other), c_ssem.at[base + other], c_rsem.at[base + other], other * 2 + core).wait_recv()
        remote(slot(core, other), slot(core, other), c_ssem.at[base2 + other], c_rsem.at[base2 + other], sibling).start()
        return carry

    lax.fori_loop(1, chips, pass_on, 0)

    def collect(k, carry):
        other = lax.rem(chip + chips - k, chips)
        remote(slot(1 - core, other), slot(1 - core, other), c_ssem.at[base2 + other], c_rsem.at[base2 + other], sibling).wait_recv()
        return carry

    lax.fori_loop(0, chips, collect, 0)
    for k in range(parts):
        tap_out[k * LANES : (k + 1) * LANES, :] = jnp.transpose(gathered[k * span : (k + 1) * span, :])

    edge_copy.wait_send()
    swap.wait_send()
    sent(0, send1, recv1, block)
    sent(1, send2, recv2, block_wide)
    sent(2, send3, recv3, block)
    sent(3, send4, recv4, block)

    def left(k, carry):
        other = lax.rem(chip + k, chips)
        remote(rows_of(half, other, piece), rows_of(rs2, other, piece), c_ssem.at[1 + other], c_rsem.at[1 + other], sibling).wait_send()
        remote(mine_sum, slot(core, other), c_ssem.at[base + other], c_rsem.at[base + other], sibling).wait_send()
        return carry

    lax.fori_loop(1, chips, left, 0)

    def handed(k, carry):
        other = lax.rem(chip + chips - k, chips)
        remote(slot(core, other), slot(core, other), c_ssem.at[base2 + other], c_rsem.at[base2 + other], sibling).wait_send()
        return carry

    lax.fori_loop(1, chips, handed, 0)
    remote(mine_sum, slot(core, chip), c_ssem.at[base2 + chip], c_rsem.at[base2 + chip], sibling).wait_send()


def fused(launch, target, taps, coupling, delay, curv):
    two, modes, length = launch.shape
    parts = lax.axis_size("tm")
    span = taps.shape[-1]
    outer = span // INNER
    rows = length // LANES
    held = modes // parts
    wide = (rows + 2) * parts * held * 2
    plain = rows * parts * held * 2
    ext = (rows + 1) * LANES
    chips = parts // 2
    size = outer * 2 * modes
    cols = INNER * modes
    tables_ = [jnp.asarray(table) for table in dft_tables(parts, rows, held)]
    vmem = pl.BlockSpec(memory_space=pltpu.VMEM)
    smem = pl.BlockSpec(memory_space=pltpu.SMEM)
    f32, bf16 = jnp.float32, jnp.bfloat16
    field = lambda n: pltpu.VMEM((n, LANES), f32)
    misfit, launch_grad, tap = pl.pallas_call(
        functools.partial(kernel, parts),
        out_shape=(
            jax.ShapeDtypeStruct((2, modes, length), f32),
            jax.ShapeDtypeStruct((2, modes, length), f32),
            jax.ShapeDtypeStruct((2 * modes * modes, span), f32),
        ),
        in_specs=[vmem] * 3 + [smem] * 2 + [pl.BlockSpec(memory_space=pltpu.HBM)] * (1 + len(tables_)),
        out_specs=(vmem, vmem, vmem),
        scratch_shapes=[
            pltpu.VMEM((2 * modes * modes, span), f32),
            *[pltpu.VMEM(table.shape, table.dtype) for table in tables_],
            field(plain), field(plain), field(wide), field(wide), field(plain), field(plain), field(plain), field(plain),
            field(2 * modes), field(2 * modes),
            pltpu.VMEM((size, cols), f32), pltpu.VMEM((size // 2, cols), f32), pltpu.VMEM((size // 2, cols), f32),
            pltpu.VMEM((size // 2, cols), f32), pltpu.VMEM((span, LANES), f32), pltpu.VMEM((parts * span, LANES), f32),
            pltpu.VMEM((span, LANES), f32), pltpu.VMEM((cols // LANES * size, LANES), f32),
            pltpu.VMEM((size, cols), bf16), pltpu.VMEM((size, cols), bf16),
            pltpu.VMEM((cols, size), bf16), pltpu.VMEM((cols, size), bf16),
            pltpu.VMEM((cols, 2 * ext), bf16), pltpu.VMEM((cols, 2 * ext), bf16),
            pltpu.VMEM((size, 2 * ext), f32),
            pltpu.VMEM((size, 2 * ext), bf16), pltpu.VMEM((size, 2 * ext), bf16),
            pltpu.VMEM((cols, 2 * ext), f32),
            pltpu.SemaphoreType.DMA((4, parts)), pltpu.SemaphoreType.DMA((4, parts)),
            pltpu.SemaphoreType.DMA, pltpu.SemaphoreType.DMA,
            pltpu.SemaphoreType.DMA((1 + 3 * chips,)), pltpu.SemaphoreType.DMA((1 + 3 * chips,)),
            pltpu.SemaphoreType.DMA((1 + len(tables_),)),
        ],
        compiler_params=pltpu.CompilerParams(collective_id=0, has_side_effects=True, vmem_limit_bytes=48 * 1024 * 1024),
    )(launch, target, coupling, delay, curv, taps.reshape(2 * modes * modes, span), *tables_)
    return misfit, launch_grad, tap.reshape(taps.shape)


def fits(launch, taps, parts):
    two, modes, length = launch.shape
    return (
        parts % 2 == 0
        and parts > 2
        and modes % parts == 0
        and modes % 16 == 0
        and length % LANES == 0
        and length * parts == WIN
        and LANES % modes == 0
        and INNER % (LANES // modes) == 0
        and taps.shape[-1] == INNER * 8
        and 2 * modes == parts * (LANES // modes)
        and (2 * (modes // parts) * (length // LANES)) % 8 == 0
        and (2 * (modes // parts) * (length // LANES + 2)) % 8 == 0
    )


def choose(launch, target, taps, coupling, delay, curv):
    if fits(launch, taps, lax.axis_size("tm")):
        return fused(launch, target, taps, coupling, delay, curv)
    return per_device(launch, target, taps, coupling, delay, curv)


def solution(mesh):
    in_specs = (P(None, None, ("grp", "tm")), P(None, None, ("grp", "tm")), P(), P(), P(), P())
    out_specs = (
        P(None, None, ("grp", "tm")),
        P(None, None, ("grp", "tm")),
        P("grp", None, None, None),
    )
    return jax.shard_map(
        choose, mesh=mesh, in_specs=in_specs, out_specs=out_specs, check_vma=False
    )
```
